32 devices in a mesh: groups: 2 (over y), node: 4 (over z), feat: 4 (over x, core).
Axes of the slice: x: 2, y: 2, z: 4, core: 2. Of those that a mesh axis runs over, the one named last changes fastest.
Arguments:
- features: bfloat16 [12288, 256], P(('groups', 'node'), 'feat'), parts along dimension 0, may hold values from -6 to 6
- tiles: bfloat16 [96, 8, 128, 128], P(('groups', 'node')), parts along dimension 0, may hold values from 0 to 0.0625
- col_block: int32 [96, 8], P(('groups', 'node')), parts along dimension 0, may hold values from 0 to 47, as said below
- weight: bfloat16 [256, 172], replicated, may hold values from -0.375 to 0.375
- bias: float32 [172], replicated, may hold values from -1 to 1
Outputs:
- logits: bfloat16 [12288, 172], P(('groups', 'node', 'feat')), parts along dimension 0
The draws below stay inside these ranges and needn't reach their ends.
There are 2 independent parts, one for each index of `groups`. The reference program is written for one: setup_inputs(seed, part) draws one part's arguments, and reference() takes and returns one part's arrays. A program takes and returns all parts, laid end to end along the dimension named above; an argument that names none is the same for every part. Nothing has to cross between parts.
Inputs may be any that keep to these rules, and one draw needn't show every extreme that they name: `col_block`: stripe d holds block rows d * 12 to (d + 1) * 12 - 1. Slot 0 of block row r is r itself; every other slot names a block of another stripe. Over the block rows of one stripe, at most 28 slots name blocks of any one other stripe, and exactly 28 name blocks of some other stripe. The same block may be named more than once.
All inputs are finite; a program needn't handle non-finite values.
Results may differ from the reference program's by a relative error of at most 0.0046.
Values may be sent and summed in bfloat16 or wider, within the bound.
No kernel may reach another device: no remote copies, remote signals or barrier semaphores. Data moves between devices by JAX's collectives and lax.ppermute only.
A program may use at most 128 MiB of HBM per device.

```python
import jax
import jax.numpy as jnp
from jax import lax

HID = 256
CLASSES = 172
BLOCK = 128
K = 8
SB = 12
NB = 48
NODES = 6144
REMOTE = 84
MAXB = 28
N_NODE = 4


def draw_col_block(key, part):

    def one_stripe(stripe):
        stripe_key = jax.random.fold_in(key, stripe + 7919)
        key_star, key_pool, key_order, key_local = jax.random.split(stripe_key, 4)
        star_offset = jax.random.randint(key_star, (), 1, N_NODE).astype(jnp.int32)
        pool_ids = jax.random.permutation(key_pool, (N_NODE - 2) * MAXB)[:REMOTE - MAXB].astype(jnp.int32)
        others = 1 + pool_ids // MAXB
        others = others + (others >= star_offset).astype(jnp.int32)
        offsets = jnp.concatenate([jnp.full((MAXB,), star_offset, jnp.int32), others.astype(jnp.int32)])
        offsets = offsets[jax.random.permutation(key_order, REMOTE)]
        local_ids = jax.random.randint(key_local, (REMOTE,), 0, SB).astype(jnp.int32)
        source = (stripe + offsets) % N_NODE
        remote = (source * SB + local_ids).reshape(SB, K - 1)
        diagonal = stripe * SB + jnp.arange(SB, dtype=jnp.int32)
        return jnp.concatenate([diagonal[:, None], remote], axis=1).astype(jnp.int32)
    stacked = jax.vmap(one_stripe)(jnp.arange(N_NODE, dtype=jnp.int32))
    return stacked.reshape(NB, K)


def level_of(key, shape, cuts, low, largest):
    factor_of = 1.0
    for axis_at, parts in cuts:
        heights = jax.random.uniform(jax.random.fold_in(jax.random.fold_in(key, 6), axis_at), (parts,), jnp.float32, low / len(cuts), largest / len(cuts))
        factor_of = factor_of * jnp.repeat(jnp.exp(heights), shape[axis_at] // parts).reshape((-1,) + (1,) * (len(shape) - 1 - axis_at))
    return factor_of


def scatter_about(own_key, extent, width, most, cuts=(), kind=jnp.bfloat16):
    values = jax.random.normal(own_key, extent, jnp.float32) * width
    if len(cuts) > 0:
        values = level_of(own_key, extent, cuts, -0.22, 0.18) * values
    return jnp.clip(values, min=-most, max=most).astype(kind)


def setup_inputs(seed: int = 0, part: int = 0) -> dict:
    splits = jax.random.split(jax.random.key(seed), 6)
    part_splits = jax.random.split(jax.random.fold_in(splits[5], part), 6)
    features = scatter_about(part_splits[0], (NODES, HID), 1.0, 6.0, ((0, 4), (1, 4)))
    tiles = jnp.clip(0.0625 * jax.random.uniform(part_splits[1], (NB, K, BLOCK, BLOCK), jnp.float32) ** level_of(part_splits[1], (NB, K, BLOCK, BLOCK), ((0, 4),), -0.2, 0.2), 0.0, 0.0625).astype(jnp.bfloat16)
    col_block = draw_col_block(jax.random.fold_in(jax.random.fold_in(splits[5], part), 71), part)
    weight = scatter_about(splits[3], (HID, CLASSES), HID ** -0.5, 0.375)
    bias = jnp.clip(jax.random.uniform(splits[4], (CLASSES,), jnp.float32, -1.0, 1.0), -1.0, 1.0)
    return dict(features=features, tiles=tiles, col_block=col_block, weight=weight, bias=bias)


def reference(features, tiles, col_block, weight, bias):
    blocks = features.reshape(NB, BLOCK, HID)

    def one_stripe(inputs):
        tile_rows, col_rows = inputs
        picked = blocks[col_rows.astype(jnp.int32)].astype(jnp.float32)
        summed = jnp.einsum("rkij,rkjf->rif", tile_rows.astype(jnp.float32), picked)
        return summed.astype(jnp.bfloat16)

    aggregated = lax.map(one_stripe, (tiles.reshape(N_NODE, SB, K, BLOCK, BLOCK), col_block.reshape(N_NODE, SB, K)))
    aggregated = aggregated.reshape(NODES, HID)
    logits = jnp.dot(aggregated, weight, preferred_element_type=jnp.float32) + bias
    return logits.astype(jnp.bfloat16)
```

```python
import functools

import jax
import jax.numpy as jnp
from jax import lax
from jax.experimental import pallas as pl
from jax.experimental.pallas import tpu as pltpu
from jax.sharding import PartitionSpec as P

VMEM = pl.BlockSpec(memory_space=pltpu.VMEM)
SMEM = pl.BlockSpec(memory_space=pltpu.SMEM)


def times_tile(block_t, tile):
    return lax.dot_general(
        block_t, tile, (((1,), (1,)), ((), ())), preferred_element_type=jnp.float32
    )


def own_kernel(me_ref, col_ref, x_ref, tiles_ref, acc_ref, list_ref, count):
    slot_count, stripe_blocks = col_ref.shape
    size = tiles_ref.shape[-1]
    sources, _ = list_ref.shape
    for source in range(sources):
        count[source] = 0
    for row in range(stripe_blocks):
        for slot in range(1, slot_count):
            column = col_ref[slot, row]
            stripe = lax.div(column, stripe_blocks)
            which = (stripe ^ me_ref[0]) - 1
            at = count[which]
            list_ref[which, at] = (row * slot_count + slot) * stripe_blocks + (
                column - stripe * stripe_blocks
            )
            count[which] = at + 1
    for row in range(stripe_blocks):
        acc_ref[row] = times_tile(
            x_ref[:, row * size : (row + 1) * size], tiles_ref[row * slot_count]
        )


def add_slots(which, list_ref, x_ref, tiles_ref, acc_ref):
    stripe_blocks = acc_ref.shape[0]
    slot_count = tiles_ref.shape[0] // stripe_blocks
    size = tiles_ref.shape[-1]
    for entry in range(list_ref.shape[1]):
        code = list_ref[which, entry]
        slot = lax.div(code, stripe_blocks)
        column = code - slot * stripe_blocks
        block = x_ref[:, pl.ds(pl.multiple_of(column * size, size), size)]
        acc_ref[lax.div(slot, slot_count)] += times_tile(block, tiles_ref[slot])


def middle_kernel(list_ref, one_ref, two_ref, tiles_ref, acc_in, acc_ref):
    del acc_in
    add_slots(0, list_ref, one_ref, tiles_ref, acc_ref)
    add_slots(1, list_ref, two_ref, tiles_ref, acc_ref)


def last_kernel(feat_ref, list_ref, three_ref, tiles_ref, acc_in, acc_ref, *part_refs):
    del acc_in
    add_slots(2, list_ref, three_ref, tiles_ref, acc_ref)
    size = tiles_ref.shape[-1]
    share = acc_ref.shape[0] // len(part_refs)
    for k, part_ref in enumerate(part_refs):
        owner = feat_ref[0] ^ k
        for row in range(share):
            part_ref[:, row * size : (row + 1) * size] = acc_ref[
                owner * share + row
            ].astype(part_ref.dtype)


def project_kernel(feat_ref, weight_ref, bias_ref, *refs):
    part_refs, out_ref, rows = refs[:-2], refs[-2], refs[-1]
    width = part_refs[0].shape[0]
    for k, part_ref in enumerate(part_refs):
        owner = feat_ref[0] ^ k
        rows[pl.ds(pl.multiple_of(owner * width, width), width), :] = part_ref[...]
    total = jnp.dot(weight_ref[...], rows[...], preferred_element_type=jnp.float32)
    out_ref[...] = (total + bias_ref[...]).astype(out_ref.dtype)


def exchange(x, axis, size, bit):
    return lax.ppermute(x, axis, [(i, i ^ bit) for i in range(size)])


def on_line(stripes, slices, features, tiles, col_block, weight, bias):
    stripe_blocks, slot_count, size, _ = tiles.shape
    width = features.shape[1]
    remote = stripe_blocks * (slot_count - 1) // (stripes - 1)
    me = lax.axis_index("node").astype(jnp.int32).reshape(1)
    feat = lax.axis_index("feat").astype(jnp.int32).reshape(1)
    x = features.T
    two = exchange(x, "node", stripes, 2)
    one = exchange(x, "node", stripes, 1)
    three = exchange(two, "node", stripes, 1)

    params = pltpu.CompilerParams(vmem_limit_bytes=32 << 20)
    acc_shape = jax.ShapeDtypeStruct((stripe_blocks, width, size), jnp.float32)
    flat = tiles.reshape(-1, size, size)
    tile_flops = 2 * size * size * width
    acc, lists = pl.pallas_call(
        own_kernel,
        out_shape=(
            acc_shape,
            jax.ShapeDtypeStruct((stripes - 1, remote), jnp.int32),
        ),
        in_specs=[SMEM, SMEM, VMEM, VMEM],
        out_specs=(VMEM, SMEM),
        scratch_shapes=[pltpu.SMEM((stripes - 1,), jnp.int32)],
        compiler_params=params,
        cost_estimate=pl.CostEstimate(
            flops=stripe_blocks * tile_flops, bytes_accessed=flat.size * 4, transcendentals=0
        ),
        name="own",
    )(me, col_block.T, x, flat)
    acc = pl.pallas_call(
        middle_kernel,
        out_shape=acc_shape,
        in_specs=[SMEM, VMEM, VMEM, VMEM, VMEM],
        out_specs=VMEM,
        input_output_aliases={4: 0},
        compiler_params=params,
        cost_estimate=pl.CostEstimate(
            flops=2 * remote * tile_flops, bytes_accessed=flat.size * 4, transcendentals=0
        ),
        name="middle",
    )(lists, one, two, flat, acc)
    part_shape = jax.ShapeDtypeStruct((width, stripe_blocks // slices * size), jnp.bfloat16)
    _, *parts = pl.pallas_call(
        last_kernel,
        out_shape=(acc_shape,) + (part_shape,) * slices,
        in_specs=[SMEM, SMEM, VMEM, VMEM, VMEM],
        out_specs=(VMEM,) * (1 + slices),
        input_output_aliases={4: 0},
        compiler_params=params,
        cost_estimate=pl.CostEstimate(
            flops=remote * tile_flops, bytes_accessed=flat.size, transcendentals=0
        ),
        name="last",
    )(feat, lists, three, flat, acc)
    parts = parts[:1] + [exchange(parts[k], "feat", slices, k) for k in range(1, slices)]
    rows = part_shape.shape[1]
    classes = weight.shape[1]
    logits = pl.pallas_call(
        project_kernel,
        out_shape=jax.ShapeDtypeStruct((classes, rows), jnp.bfloat16),
        in_specs=[SMEM] + [VMEM] * (2 + slices),
        out_specs=VMEM,
        scratch_shapes=[pltpu.VMEM((slices * width, rows), jnp.bfloat16)],
        compiler_params=params,
        name="project",
    )(feat, weight.T, bias[:, None], *parts)
    return logits.T


def on_device(features, tiles, col_block, weight, bias):
    stripe_blocks, slot_count, size, _ = tiles.shape
    width = features.shape[1]
    gathered = lax.all_gather(features, "node", axis=0, tiled=True)
    fetched = gathered.reshape(-1, size, width)[col_block.reshape(-1)]
    fetched = fetched.reshape(stripe_blocks, slot_count, size, width)
    summed = jnp.einsum("rkij,rkjf->rif", tiles, fetched, preferred_element_type=jnp.float32)
    aggregated = summed.astype(jnp.bfloat16).reshape(-1, width)
    rows = lax.all_to_all(aggregated, "feat", split_axis=0, concat_axis=1, tiled=True)
    logits = jnp.dot(rows, weight, preferred_element_type=jnp.float32)
    return (logits + bias).astype(jnp.bfloat16)


def solution(mesh):
    stripes, slices = mesh.shape["node"], mesh.shape["feat"]
    line = stripes == 4 and slices & (slices - 1) == 0
    body = functools.partial(on_line, stripes, slices) if line else on_device
    in_specs = (
        P(("groups", "node"), "feat"),
        P(("groups", "node"), None, None, None),
        P(("groups", "node"), None),
        P(),
        P(),
    )
    out_specs = P(("groups", "node", "feat"), None)
    return jax.shard_map(
        body, mesh=mesh, in_specs=in_specs, out_specs=out_specs, check_vma=False
    )
```

```python
import functools

import jax
import jax.numpy as jnp
from jax import lax
from jax.experimental import pallas as pl
from jax.experimental.pallas import tpu as pltpu
from jax.sharding import PartitionSpec as P

VMEM = pl.BlockSpec(memory_space=pltpu.VMEM)
HBM = pl.BlockSpec(memory_space=pltpu.HBM)
SMEM = pl.BlockSpec(memory_space=pltpu.SMEM)


def times_tile(block_t, tile):
    return lax.dot_general(
        block_t, tile, (((1,), (1,)), ((), ())), preferred_element_type=jnp.float32
    )


def own_kernel(
    me_ref, col_ref, x_hbm, tiles_hbm, acc_ref, list_ref, x_ref, tiles_ref, count, sems
):
    slot_count, stripe_blocks = col_ref.shape
    size = tiles_ref.shape[-1]
    copies = [
        pltpu.make_async_copy(x_hbm, x_ref, sems.at[0]),
        pltpu.make_async_copy(tiles_hbm.at[:, 0], tiles_ref, sems.at[1]),
    ]
    for copy in copies:
        copy.start()
    for source in range(list_ref.shape[0]):
        count[source] = 0
    for row in range(stripe_blocks):
        for slot in range(1, slot_count):
            column = col_ref[slot, row]
            stripe = lax.div(column, stripe_blocks)
            which = (stripe ^ me_ref[0]) - 1
            at = count[which]
            list_ref[which, at] = (row * slot_count + slot) * stripe_blocks + (
                column - stripe * stripe_blocks
            )
            count[which] = at + 1
    for copy in copies:
        copy.wait()
    for row in range(stripe_blocks):
        acc_ref[row] = times_tile(x_ref[:, row * size : (row + 1) * size], tiles_ref[row])


def add_slots(which, list_ref, x_ref, tiles, acc_ref, slot_count):
    stripe_blocks = acc_ref.shape[0]
    size = tiles.shape[-1]
    for entry in range(list_ref.shape[1]):
        code = list_ref[which, entry]
        slot = lax.div(code, stripe_blocks)
        column = code - slot * stripe_blocks
        block = x_ref[:, pl.ds(pl.multiple_of(column * size, size), size)]
        acc_ref[lax.div(slot, slot_count)] += times_tile(block, tiles[entry])


def middle_kernel(
    list_ref, one_ref, two_ref, tiles_hbm, acc_in, acc_ref, three_tiles, tiles_ref, sems
):
    del acc_in
    stripe_blocks, slot_count = tiles_hbm.shape[:2]
    slots = list_ref.shape[1]
    places = [tiles_ref.at[0], tiles_ref.at[1], three_tiles]
    for which, place in enumerate(places):
        for entry in range(slots):
            slot = lax.div(list_ref[which, entry], stripe_blocks)
            row = lax.div(slot, slot_count)
            pltpu.make_async_copy(
                tiles_hbm.at[row, slot - row * slot_count], place.at[entry], sems.at[which]
            ).start()
    for which, x_ref in enumerate([one_ref, two_ref]):
        place = places[which]
        pltpu.make_async_copy(place, place, sems.at[which]).wait()
        add_slots(which, list_ref, x_ref, place, acc_ref, slot_count)
    pltpu.make_async_copy(three_tiles, three_tiles, sems.at[2]).wait()


def last_kernel(slot_count, feat_ref, list_ref, three_ref, tiles_ref, acc_in, acc_ref, *part_refs):
    del acc_in
    add_slots(2, list_ref, three_ref, tiles_ref, acc_ref, slot_count)
    size = tiles_ref.shape[-1]
    share = acc_ref.shape[0] // len(part_refs)
    for k, part_ref in enumerate(part_refs):
        owner = feat_ref[0] ^ k
        for row in range(share):
            part_ref[:, row * size : (row + 1) * size] = acc_ref[
                owner * share + row
            ].astype(part_ref.dtype)


def project_kernel(feat_ref, weight_ref, bias_ref, *refs):
    part_refs, out_ref, rows = refs[:-2], refs[-2], refs[-1]
    width = part_refs[0].shape[0]
    for k, part_ref in enumerate(part_refs):
        owner = feat_ref[0] ^ k
        rows[pl.ds(pl.multiple_of(owner * width, width), width), :] = part_ref[...]
    total = jnp.dot(weight_ref[...], rows[...], preferred_element_type=jnp.float32)
    out_ref[...] = (total + bias_ref[...]).astype(out_ref.dtype)


def in_hbm(x):
    return pltpu.with_memory_space_constraint(x, pltpu.HBM)


def in_vmem(*arrays):
    return [pltpu.with_memory_space_constraint(x, pltpu.VMEM) for x in arrays]


def exchange(x, axis, size, bit):
    return lax.ppermute(x, axis, [(i, i ^ bit) for i in range(size)])


def on_line(stripes, slices, features, tiles, col_block, weight, bias):
    stripe_blocks, slot_count, size, _ = tiles.shape
    width = features.shape[1]
    remote = stripe_blocks * (slot_count - 1) // (stripes - 1)
    me = lax.axis_index("node").astype(jnp.int32).reshape(1)
    feat = lax.axis_index("feat").astype(jnp.int32).reshape(1)
    x = features.T
    two = exchange(x, "node", stripes, 2)
    one = exchange(x, "node", stripes, 1)

    params = pltpu.CompilerParams(vmem_limit_bytes=12 << 20)
    acc_shape = pltpu.VMEM((stripe_blocks, width, size), jnp.float32)
    tile_flops = 2 * size * size * width
    held = pltpu.VMEM((remote, size, size), tiles.dtype)
    acc, lists = pl.pallas_call(
        own_kernel,
        out_shape=(acc_shape, jax.ShapeDtypeStruct((stripes - 1, remote), jnp.int32)),
        in_specs=[SMEM, SMEM, HBM, HBM],
        out_specs=(VMEM, SMEM),
        scratch_shapes=[
            pltpu.VMEM(x.shape, x.dtype),
            pltpu.VMEM((stripe_blocks, size, size), tiles.dtype),
            pltpu.SMEM((stripes - 1,), jnp.int32),
            pltpu.SemaphoreType.DMA((2,)),
        ],
        compiler_params=params,
        cost_estimate=pl.CostEstimate(
            flops=stripe_blocks * tile_flops, bytes_accessed=tiles.size, transcendentals=0
        ),
        name="own",
    )(me, col_block.T, in_hbm(x), in_hbm(tiles))
    ready, acc = lax.optimization_barrier((two, acc))
    three = exchange(ready, "node", stripes, 1)
    acc, three_tiles = pl.pallas_call(
        middle_kernel,
        out_shape=(acc_shape, held),
        in_specs=[SMEM, VMEM, VMEM, HBM, VMEM],
        out_specs=(VMEM, VMEM),
        input_output_aliases={4: 0},
        scratch_shapes=[
            pltpu.VMEM((2,) + held.shape, held.dtype),
            pltpu.SemaphoreType.DMA((3,)),
        ],
        compiler_params=params,
        cost_estimate=pl.CostEstimate(
            flops=2 * remote * tile_flops, bytes_accessed=tiles.size * 4, transcendentals=0
        ),
        name="middle",
    )(lists, *in_vmem(one, ready), in_hbm(tiles), *in_vmem(acc))
    part_shape = pltpu.VMEM((width, stripe_blocks // slices * size), jnp.bfloat16)
    _, *parts = pl.pallas_call(
        functools.partial(last_kernel, slot_count),
        out_shape=(acc_shape,) + (part_shape,) * slices,
        in_specs=[SMEM, SMEM, VMEM, VMEM, VMEM],
        out_specs=(VMEM,) * (1 + slices),
        input_output_aliases={4: 0},
        compiler_params=params,
        cost_estimate=pl.CostEstimate(
            flops=remote * tile_flops, bytes_accessed=tiles.size, transcendentals=0
        ),
        name="last",
    )(feat, lists, *in_vmem(three, three_tiles, acc))
    parts = parts[:1] + [
        exchange(parts[k], "feat", slices, k) for k in range(1, slices)
    ]
    rows = part_shape.shape[1]
    classes = weight.shape[1]
    logits = pl.pallas_call(
        project_kernel,
        out_shape=jax.ShapeDtypeStruct((classes, rows), jnp.bfloat16),
        in_specs=[SMEM] + [VMEM] * (2 + slices),
        out_specs=VMEM,
        scratch_shapes=[pltpu.VMEM((slices * width, rows), jnp.bfloat16)],
        compiler_params=params,
        name="project",
    )(feat, *in_vmem(weight.T, bias[:, None], *parts))
    return logits.T


def on_device(features, tiles, col_block, weight, bias):
    stripe_blocks, slot_count, size, _ = tiles.shape
    width = features.shape[1]
    gathered = lax.all_gather(features, "node", axis=0, tiled=True)
    fetched = gathered.reshape(-1, size, width)[col_block.reshape(-1)]
    fetched = fetched.reshape(stripe_blocks, slot_count, size, width)
    summed = jnp.einsum("rkij,rkjf->rif", tiles, fetched, preferred_element_type=jnp.float32)
    aggregated = summed.astype(jnp.bfloat16).reshape(-1, width)
    rows = lax.all_to_all(aggregated, "feat", split_axis=0, concat_axis=1, tiled=True)
    logits = jnp.dot(rows, weight, preferred_element_type=jnp.float32)
    return (logits + bias).astype(jnp.bfloat16)


def solution(mesh):
    stripes, slices = mesh.shape["node"], mesh.shape["feat"]
    line = stripes == 4 and slices > 1 and slices & (slices - 1) == 0
    body = functools.partial(on_line, stripes, slices) if line else on_device
    in_specs = (
        P(("groups", "node"), "feat"),
        P(("groups", "node"), None, None, None),
        P(("groups", "node"), None),
        P(),
        P(),
    )
    out_specs = P(("groups", "node", "feat"), None)
    return jax.shard_map(
        body, mesh=mesh, in_specs=in_specs, out_specs=out_specs, check_vma=False
    )
```

```python
import functools

import jax
import jax.numpy as jnp
from jax import lax
from jax.experimental import pallas as pl
from jax.experimental.pallas import tpu as pltpu
from jax.sharding import PartitionSpec as P

VMEM = pl.BlockSpec(memory_space=pltpu.VMEM)
HBM = pl.BlockSpec(memory_space=pltpu.HBM)
SMEM = pl.BlockSpec(memory_space=pltpu.SMEM)


def times_tile(block_t, tile):
    return lax.dot_general(
        block_t, tile, (((1,), (1,)), ((), ())), preferred_element_type=jnp.float32
    )


def own_kernel(
    me_ref, col_ref, x_hbm, tiles_hbm, acc_ref, list_ref, x_ref, tiles_ref, count, sems
):
    slot_count, stripe_blocks = col_ref.shape
    size = tiles_ref.shape[-1]
    copies = [
        pltpu.make_async_copy(x_hbm, x_ref, sems.at[0]),
        pltpu.make_async_copy(tiles_hbm.at[:, 0], tiles_ref, sems.at[1]),
    ]
    for copy in copies:
        copy.start()
    for source in range(list_ref.shape[0]):
        count[source] = 0
    for row in range(stripe_blocks):
        for slot in range(1, slot_count):
            column = col_ref[slot, row]
            stripe = lax.div(column, stripe_blocks)
            which = (stripe ^ me_ref[0]) - 1
            at = count[which]
            list_ref[which, at] = (row * slot_count + slot) * stripe_blocks + (
                column - stripe * stripe_blocks
            )
            count[which] = at + 1
    for copy in copies:
        copy.wait()
    for row in range(stripe_blocks):
        acc_ref[row] = times_tile(x_ref[:, row * size : (row + 1) * size], tiles_ref[row])


def times_turned(block_t, tile_t):
    return jnp.dot(block_t, tile_t, preferred_element_type=jnp.float32)


def add_slots(which, list_ref, x_ref, tiles, acc_ref, slot_count, times):
    stripe_blocks = acc_ref.shape[0]
    size = tiles.shape[-1]
    for entry in range(list_ref.shape[1]):
        code = list_ref[which, entry]
        slot = lax.div(code, stripe_blocks)
        column = code - slot * stripe_blocks
        block = x_ref[:, pl.ds(pl.multiple_of(column * size, size), size)]
        acc_ref[lax.div(slot, slot_count)] += times(block, tiles[entry])


def middle_kernel(
    list_ref, one_ref, two_ref, tiles_hbm, acc_in, acc_ref, three_tiles, tiles_ref, sems
):
    del acc_in
    stripe_blocks, slot_count = tiles_hbm.shape[:2]
    slots = list_ref.shape[1]
    places = [tiles_ref.at[0], tiles_ref.at[1], tiles_ref.at[2]]
    for which, place in enumerate(places):
        for entry in range(slots):
            slot = lax.div(list_ref[which, entry], stripe_blocks)
            row = lax.div(slot, slot_count)
            pltpu.make_async_copy(
                tiles_hbm.at[row, slot - row * slot_count], place.at[entry], sems.at[which]
            ).start()
    for which, x_ref in enumerate([one_ref, two_ref]):
        place = places[which]
        pltpu.make_async_copy(place, place, sems.at[which]).wait()
        add_slots(which, list_ref, x_ref, place, acc_ref, slot_count, times_tile)
    pltpu.make_async_copy(places[2], places[2], sems.at[2]).wait()
    for entry in range(slots):
        three_tiles[entry] = places[2][entry].T


def last_kernel(slot_count, feat_ref, list_ref, three_ref, tiles_ref, acc_in, acc_ref, *part_refs):
    del acc_in
    add_slots(2, list_ref, three_ref, tiles_ref, acc_ref, slot_count, times_turned)
    size = tiles_ref.shape[-1]
    share = acc_ref.shape[0] // len(part_refs)
    for k, part_ref in enumerate(part_refs):
        owner = feat_ref[0] ^ k
        for row in range(share):
            part_ref[:, row * size : (row + 1) * size] = acc_ref[
                owner * share + row
            ].astype(part_ref.dtype)


def project_kernel(feat_ref, weight_ref, bias_ref, *refs):
    part_refs, out_ref, rows = refs[:-2], refs[-2], refs[-1]
    width = part_refs[0].shape[0]
    for k, part_ref in enumerate(part_refs):
        owner = feat_ref[0] ^ k
        rows[pl.ds(pl.multiple_of(owner * width, width), width), :] = part_ref[...]
    total = jnp.dot(weight_ref[...], rows[...], preferred_element_type=jnp.float32)
    out_ref[...] = (total + bias_ref[...]).astype(out_ref.dtype)


def in_hbm(x):
    return pltpu.with_memory_space_constraint(x, pltpu.HBM)


def in_vmem(*arrays):
    return [pltpu.with_memory_space_constraint(x, pltpu.VMEM) for x in arrays]


def exchange(x, axis, size, bit):
    return lax.ppermute(x, axis, [(i, i ^ bit) for i in range(size)])


def on_line(stripes, slices, features, tiles, col_block, weight, bias):
    stripe_blocks, slot_count, size, _ = tiles.shape
    width = features.shape[1]
    remote = stripe_blocks * (slot_count - 1) // (stripes - 1)
    me = lax.axis_index("node").astype(jnp.int32).reshape(1)
    feat = lax.axis_index("feat").astype(jnp.int32).reshape(1)
    x = features.T
    two = exchange(x, "node", stripes, 2)
    one = exchange(x, "node", stripes, 1)

    params = pltpu.CompilerParams(vmem_limit_bytes=12 << 20)
    acc_shape = pltpu.VMEM((stripe_blocks, width, size), jnp.float32)
    tile_flops = 2 * size * size * width
    held = pltpu.VMEM((remote, size, size), tiles.dtype)
    acc, lists = pl.pallas_call(
        own_kernel,
        out_shape=(acc_shape, jax.ShapeDtypeStruct((stripes - 1, remote), jnp.int32)),
        in_specs=[SMEM, SMEM, HBM, HBM],
        out_specs=(VMEM, SMEM),
        scratch_shapes=[
            pltpu.VMEM(x.shape, x.dtype),
            pltpu.VMEM((stripe_blocks, size, size), tiles.dtype),
            pltpu.SMEM((stripes - 1,), jnp.int32),
            pltpu.SemaphoreType.DMA((2,)),
        ],
        compiler_params=params,
        cost_estimate=pl.CostEstimate(
            flops=stripe_blocks * tile_flops, bytes_accessed=tiles.size, transcendentals=0
        ),
        name="own",
    )(me, col_block.T, in_hbm(x), in_hbm(tiles))
    ready, acc = lax.optimization_barrier((two, acc))
    three = exchange(ready, "node", stripes, 1)
    acc, three_tiles = pl.pallas_call(
        middle_kernel,
        out_shape=(acc_shape, held),
        in_specs=[SMEM, VMEM, VMEM, HBM, VMEM],
        out_specs=(VMEM, VMEM),
        input_output_aliases={4: 0},
        scratch_shapes=[
            pltpu.VMEM((3,) + held.shape, held.dtype),
            pltpu.SemaphoreType.DMA((3,)),
        ],
        compiler_params=params,
        cost_estimate=pl.CostEstimate(
            flops=2 * remote * tile_flops, bytes_accessed=tiles.size * 4, transcendentals=0
        ),
        name="middle",
    )(lists, *in_vmem(one, ready), in_hbm(tiles), *in_vmem(acc))
    part_shape = pltpu.VMEM((width, stripe_blocks // slices * size), jnp.bfloat16)
    _, *parts = pl.pallas_call(
        functools.partial(last_kernel, slot_count),
        out_shape=(acc_shape,) + (part_shape,) * slices,
        in_specs=[SMEM, SMEM, VMEM, VMEM, VMEM],
        out_specs=(VMEM,) * (1 + slices),
        input_output_aliases={4: 0},
        compiler_params=params,
        cost_estimate=pl.CostEstimate(
            flops=remote * tile_flops, bytes_accessed=tiles.size, transcendentals=0
        ),
        name="last",
    )(feat, lists, *in_vmem(three, three_tiles, acc))
    parts = parts[:1] + [
        exchange(parts[k], "feat", slices, k) for k in range(1, slices)
    ]
    rows = part_shape.shape[1]
    classes = weight.shape[1]
    logits = pl.pallas_call(
        project_kernel,
        out_shape=jax.ShapeDtypeStruct((classes, rows), jnp.bfloat16),
        in_specs=[SMEM] + [VMEM] * (2 + slices),
        out_specs=VMEM,
        scratch_shapes=[pltpu.VMEM((slices * width, rows), jnp.bfloat16)],
        compiler_params=params,
        name="project",
    )(feat, *in_vmem(weight.T, bias[:, None], *parts))
    return logits.T


def on_device(features, tiles, col_block, weight, bias):
    stripe_blocks, slot_count, size, _ = tiles.shape
    width = features.shape[1]
    gathered = lax.all_gather(features, "node", axis=0, tiled=True)
    fetched = gathered.reshape(-1, size, width)[col_block.reshape(-1)]
    fetched = fetched.reshape(stripe_blocks, slot_count, size, width)
    summed = jnp.einsum("rkij,rkjf->rif", tiles, fetched, preferred_element_type=jnp.float32)
    aggregated = summed.astype(jnp.bfloat16).reshape(-1, width)
    rows = lax.all_to_all(aggregated, "feat", split_axis=0, concat_axis=1, tiled=True)
    logits = jnp.dot(rows, weight, preferred_element_type=jnp.float32)
    return (logits + bias).astype(jnp.bfloat16)


def solution(mesh):
    stripes, slices = mesh.shape["node"], mesh.shape["feat"]
    line = stripes == 4 and slices > 1 and slices & (slices - 1) == 0
    body = functools.partial(on_line, stripes, slices) if line else on_device
    in_specs = (
        P(("groups", "node"), "feat"),
        P(("groups", "node"), None, None, None),
        P(("groups", "node"), None),
        P(),
        P(),
    )
    out_specs = P(("groups", "node", "feat"), None)
    return jax.shard_map(
        body, mesh=mesh, in_specs=in_specs, out_specs=out_specs, check_vma=False
    )
```

```python
import functools

import jax
import jax.numpy as jnp
from jax import lax
from jax.experimental import pallas as pl
from jax.experimental.pallas import tpu as pltpu
from jax.sharding import PartitionSpec as P

VMEM = pl.BlockSpec(memory_space=pltpu.VMEM)
HBM = pl.BlockSpec(memory_space=pltpu.HBM)
SMEM = pl.BlockSpec(memory_space=pltpu.SMEM)


def times_tile(block_t, tile):
    return lax.dot_general(
        block_t, tile, (((1,), (1,)), ((), ())), preferred_element_type=jnp.float32
    )


def own_kernel(
    me_ref, col_ref, x_hbm, tiles_hbm, acc_ref, list_ref, x_ref, tiles_ref, count, sems
):
    slot_count, stripe_blocks = col_ref.shape
    size = tiles_ref.shape[-1]
    copies = [
        pltpu.make_async_copy(x_hbm, x_ref, sems.at[0]),
        pltpu.make_async_copy(tiles_hbm.at[:, 0], tiles_ref, sems.at[1]),
    ]
    for copy in copies:
        copy.start()
    for source in range(list_ref.shape[0]):
        count[source] = 0
    for row in range(stripe_blocks):
        for slot in range(1, slot_count):
            column = col_ref[slot, row]
            stripe = lax.div(column, stripe_blocks)
            which = (stripe ^ me_ref[0]) - 1
            at = count[which]
            list_ref[which, at] = (row * slot_count + slot) * stripe_blocks + (
                column - stripe * stripe_blocks
            )
            count[which] = at + 1
    for copy in copies:
        copy.wait()
    for row in range(stripe_blocks):
        acc_ref[row] = times_tile(x_ref[:, row * size : (row + 1) * size], tiles_ref[row])


def times_turned(block_t, tile_t):
    return jnp.dot(block_t, tile_t, preferred_element_type=jnp.float32)


def add_slots(which, list_ref, x_ref, tiles, acc_ref, slot_count, times):
    stripe_blocks = acc_ref.shape[0]
    size = tiles.shape[-1]
    for entry in range(list_ref.shape[1]):
        code = list_ref[which, entry]
        slot = lax.div(code, stripe_blocks)
        column = code - slot * stripe_blocks
        block = x_ref[:, pl.ds(pl.multiple_of(column * size, size), size)]
        acc_ref[lax.div(slot, slot_count)] += times(block, tiles[entry])


def middle_kernel(
    list_ref, one_ref, two_ref, tiles_hbm, acc_in, acc_ref, three_tiles, tiles_ref, sems
):
    del acc_in
    stripe_blocks, slot_count = tiles_hbm.shape[:2]
    slots = list_ref.shape[1]
    places = [tiles_ref.at[0], tiles_ref.at[1], tiles_ref.at[2]]
    for which, place in enumerate(places):
        for entry in range(slots):
            slot = lax.div(list_ref[which, entry], stripe_blocks)
            row = lax.div(slot, slot_count)
            pltpu.make_async_copy(
                tiles_hbm.at[row, slot - row * slot_count], place.at[entry], sems.at[which]
            ).start()
    for which, x_ref in enumerate([one_ref, two_ref]):
        place = places[which]
        pltpu.make_async_copy(place, place, sems.at[which]).wait()
        add_slots(which, list_ref, x_ref, place, acc_ref, slot_count, times_tile)
    pltpu.make_async_copy(places[2], places[2], sems.at[2]).wait()
    for entry in range(slots):
        three_tiles[entry] = places[2][entry].T


def last_kernel(slot_count, feat_ref, list_ref, three_ref, tiles_ref, acc_in, acc_ref, *part_refs):
    del acc_in
    add_slots(2, list_ref, three_ref, tiles_ref, acc_ref, slot_count, times_turned)
    size = tiles_ref.shape[-1]
    share = acc_ref.shape[0] // len(part_refs)
    for k, part_ref in enumerate(part_refs):
        owner = feat_ref[0] ^ k
        for row in range(share):
            part_ref[:, row * size : (row + 1) * size] = acc_ref[
                owner * share + row
            ].astype(part_ref.dtype)


def project_kernel(feat_ref, weight_ref, bias_ref, *refs):
    part_refs, out_ref, rows = refs[:-2], refs[-2], refs[-1]
    width = part_refs[0].shape[0]
    for k, part_ref in enumerate(part_refs):
        owner = feat_ref[0] ^ k
        rows[pl.ds(pl.multiple_of(owner * width, width), width), :] = part_ref[...]
    total = jnp.dot(weight_ref[...], rows[...], preferred_element_type=jnp.float32)
    out_ref[...] = (total + bias_ref[...]).astype(out_ref.dtype)


def in_hbm(x):
    return pltpu.with_memory_space_constraint(x, pltpu.HBM)


def in_vmem(*arrays):
    return [pltpu.with_memory_space_constraint(x, pltpu.VMEM) for x in arrays]


def exchange(x, axis, size, bit):
    return lax.ppermute(x, axis, [(i, i ^ bit) for i in range(size)])


def on_line(stripes, slices, features, tiles, col_block, weight, bias):
    stripe_blocks, slot_count, size, _ = tiles.shape
    width = features.shape[1]
    remote = stripe_blocks * (slot_count - 1) // (stripes - 1)
    me = lax.axis_index("node").astype(jnp.int32).reshape(1)
    feat = lax.axis_index("feat").astype(jnp.int32).reshape(1)
    x = features.T
    two = exchange(x, "node", stripes, 2)
    one = exchange(x, "node", stripes, 1)

    params = pltpu.CompilerParams(vmem_limit_bytes=12 << 20)
    acc_shape = pltpu.VMEM((stripe_blocks, width, size), jnp.float32)
    tile_flops = 2 * size * size * width
    held = pltpu.VMEM((remote, size, size), tiles.dtype)
    acc, lists = pl.pallas_call(
        own_kernel,
        out_shape=(acc_shape, jax.ShapeDtypeStruct((stripes - 1, remote), jnp.int32)),
        in_specs=[SMEM, SMEM, HBM, HBM],
        out_specs=(VMEM, SMEM),
        scratch_shapes=[
            pltpu.VMEM(x.shape, x.dtype),
            pltpu.VMEM((stripe_blocks, size, size), tiles.dtype),
            pltpu.SMEM((stripes - 1,), jnp.int32),
            pltpu.SemaphoreType.DMA((2,)),
        ],
        compiler_params=params,
        cost_estimate=pl.CostEstimate(
            flops=stripe_blocks * tile_flops, bytes_accessed=tiles.size, transcendentals=0
        ),
        name="own",
    )(me, col_block.T, in_hbm(x), in_hbm(tiles))
    ready, acc = lax.optimization_barrier((two, acc))
    three = exchange(ready, "node", stripes, 1)
    acc, three_tiles = pl.pallas_call(
        middle_kernel,
        out_shape=(acc_shape, held),
        in_specs=[VMEM, VMEM, VMEM, HBM, VMEM],
        out_specs=(VMEM, VMEM),
        input_output_aliases={4: 0},
        scratch_shapes=[
            pltpu.VMEM((3,) + held.shape, held.dtype),
            pltpu.SemaphoreType.DMA((3,)),
        ],
        compiler_params=params,
        cost_estimate=pl.CostEstimate(
            flops=2 * remote * tile_flops, bytes_accessed=tiles.size * 4, transcendentals=0
        ),
        name="middle",
    )(*in_vmem(lists, one, ready), in_hbm(tiles), *in_vmem(acc))
    part_shape = pltpu.VMEM((width, stripe_blocks // slices * size), jnp.bfloat16)
    _, *parts = pl.pallas_call(
        functools.partial(last_kernel, slot_count),
        out_shape=(acc_shape,) + (part_shape,) * slices,
        in_specs=[SMEM, VMEM, VMEM, VMEM, VMEM],
        out_specs=(VMEM,) * (1 + slices),
        input_output_aliases={4: 0},
        compiler_params=params,
        cost_estimate=pl.CostEstimate(
            flops=remote * tile_flops, bytes_accessed=tiles.size, transcendentals=0
        ),
        name="last",
    )(feat, *in_vmem(lists, three, three_tiles, acc))
    parts = parts[:1] + [
        exchange(parts[k], "feat", slices, k) for k in range(1, slices)
    ]
    rows = part_shape.shape[1]
    classes = weight.shape[1]
    logits = pl.pallas_call(
        project_kernel,
        out_shape=jax.ShapeDtypeStruct((classes, rows), jnp.bfloat16),
        in_specs=[SMEM] + [VMEM] * (2 + slices),
        out_specs=VMEM,
        scratch_shapes=[pltpu.VMEM((slices * width, rows), jnp.bfloat16)],
        compiler_params=params,
        name="project",
    )(feat, *in_vmem(weight.T, bias[:, None], *parts))
    return logits.T


def on_device(features, tiles, col_block, weight, bias):
    stripe_blocks, slot_count, size, _ = tiles.shape
    width = features.shape[1]
    gathered = lax.all_gather(features, "node", axis=0, tiled=True)
    fetched = gathered.reshape(-1, size, width)[col_block.reshape(-1)]
    fetched = fetched.reshape(stripe_blocks, slot_count, size, width)
    summed = jnp.einsum("rkij,rkjf->rif", tiles, fetched, preferred_element_type=jnp.float32)
    aggregated = summed.astype(jnp.bfloat16).reshape(-1, width)
    rows = lax.all_to_all(aggregated, "feat", split_axis=0, concat_axis=1, tiled=True)
    logits = jnp.dot(rows, weight, preferred_element_type=jnp.float32)
    return (logits + bias).astype(jnp.bfloat16)


def solution(mesh):
    stripes, slices = mesh.shape["node"], mesh.shape["feat"]
    line = stripes == 4 and slices > 1 and slices & (slices - 1) == 0
    body = functools.partial(on_line, stripes, slices) if line else on_device
    in_specs = (
        P(("groups", "node"), "feat"),
        P(("groups", "node"), None, None, None),
        P(("groups", "node"), None),
        P(),
        P(),
    )
    out_specs = P(("groups", "node", "feat"), None)
    return jax.shard_map(
        body, mesh=mesh, in_specs=in_specs, out_specs=out_specs, check_vma=False
    )
```

```python
import functools

import jax
import jax.numpy as jnp
from jax import lax
from jax.experimental import pallas as pl
from jax.experimental.pallas import tpu as pltpu
from jax.sharding import PartitionSpec as P

VMEM = pl.BlockSpec(memory_space=pltpu.VMEM)
HBM = pl.BlockSpec(memory_space=pltpu.HBM)
SMEM = pl.BlockSpec(memory_space=pltpu.SMEM)


def times_tile(block_t, tile):
    return lax.dot_general(
        block_t, tile, (((1,), (1,)), ((), ())), preferred_element_type=jnp.float32
    )


def own_kernel(
    me_ref, col_ref, x_hbm, tiles_hbm, acc_ref, list_ref, x_ref, tiles_ref, count, sems
):
    slot_count, stripe_blocks = col_ref.shape
    size = tiles_ref.shape[-1]
    copies = [
        pltpu.make_async_copy(x_hbm, x_ref, sems.at[0]),
        pltpu.make_async_copy(tiles_hbm.at[:, 0], tiles_ref, sems.at[1]),
    ]
    for copy in copies:
        copy.start()
    for source in range(list_ref.shape[0]):
        count[source] = 0
    for row in range(stripe_blocks):
        for slot in range(1, slot_count):
            column = col_ref[slot, row]
            stripe = lax.div(column, stripe_blocks)
            which = (stripe ^ me_ref[0]) - 1
            at = count[which]
            list_ref[which, at] = (row * slot_count + slot) * stripe_blocks + (
                column - stripe * stripe_blocks
            )
            count[which] = at + 1
    for copy in copies:
        copy.wait()
    for row in range(stripe_blocks):
        acc_ref[row] = times_tile(x_ref[:, row * size : (row + 1) * size], tiles_ref[row])


def times_turned(block_t, tile_t):
    return jnp.dot(block_t, tile_t, preferred_element_type=jnp.float32)


def add_slots(which, list_ref, x_ref, tiles, acc_ref, slot_count, times):
    stripe_blocks = acc_ref.shape[0]
    size = tiles.shape[-1]
    for entry in range(list_ref.shape[1]):
        code = list_ref[which, entry]
        slot = lax.div(code, stripe_blocks)
        column = code - slot * stripe_blocks
        block = x_ref[:, pl.ds(pl.multiple_of(column * size, size), size)]
        acc_ref[lax.div(slot, slot_count)] += times(block, tiles[entry])


def middle_kernel(
    list_ref, one_ref, two_ref, tiles_hbm, acc_in, acc_ref, three_tiles, tiles_ref, sems
):
    del acc_in
    stripe_blocks, slot_count = tiles_hbm.shape[:2]
    slots = list_ref.shape[1]
    places = [tiles_ref.at[0], tiles_ref.at[1], tiles_ref.at[2]]
    for which, place in enumerate(places):
        for entry in range(slots):
            slot = lax.div(list_ref[which, entry], stripe_blocks)
            row = lax.div(slot, slot_count)
            pltpu.make_async_copy(
                tiles_hbm.at[row, slot - row * slot_count], place.at[entry], sems.at[which]
            ).start()
    for which, x_ref in enumerate([one_ref, two_ref]):
        place = places[which]
        pltpu.make_async_copy(place, place, sems.at[which]).wait()
        add_slots(which, list_ref, x_ref, place, acc_ref, slot_count, times_tile)
    pltpu.make_async_copy(places[2], places[2], sems.at[2]).wait()
    for entry in range(slots):
        three_tiles[entry] = places[2][entry].T


def last_kernel(slot_count, feat_ref, list_ref, three_ref, tiles_ref, acc_in, acc_ref, *part_refs):
    del acc_in
    add_slots(2, list_ref, three_ref, tiles_ref, acc_ref, slot_count, times_turned)
    size = tiles_ref.shape[-1]
    share = acc_ref.shape[0] // len(part_refs)
    for k, part_ref in enumerate(reversed(part_refs)):
        owner = feat_ref[0] ^ k
        for row in range(share):
            part_ref[:, row * size : (row + 1) * size] = acc_ref[
                owner * share + row
            ].astype(part_ref.dtype)


def project_kernel(feat_ref, weight_ref, bias_ref, *refs):
    part_refs, out_ref, rows = refs[:-2], refs[-2], refs[-1]
    width = part_refs[0].shape[0]
    for k, part_ref in enumerate(reversed(part_refs)):
        owner = feat_ref[0] ^ k
        rows[pl.ds(pl.multiple_of(owner * width, width), width), :] = part_ref[...]
    total = jnp.dot(weight_ref[...], rows[...], preferred_element_type=jnp.float32)
    out_ref[...] = (total + bias_ref[...]).astype(out_ref.dtype)


def in_hbm(x):
    return pltpu.with_memory_space_constraint(x, pltpu.HBM)


def in_vmem(*arrays):
    return [pltpu.with_memory_space_constraint(x, pltpu.VMEM) for x in arrays]


def exchange(x, axis, size, bit):
    return lax.ppermute(x, axis, [(i, i ^ bit) for i in range(size)])


def on_line(stripes, slices, features, tiles, col_block, weight, bias):
    stripe_blocks, slot_count, size, _ = tiles.shape
    width = features.shape[1]
    remote = stripe_blocks * (slot_count - 1) // (stripes - 1)
    me = lax.axis_index("node").astype(jnp.int32).reshape(1)
    feat = lax.axis_index("feat").astype(jnp.int32).reshape(1)
    x = features.T
    two = exchange(x, "node", stripes, 2)
    one = exchange(x, "node", stripes, 1)

    params = pltpu.CompilerParams(vmem_limit_bytes=12 << 20)
    acc_shape = pltpu.VMEM((stripe_blocks, width, size), jnp.float32)
    tile_flops = 2 * size * size * width
    held = pltpu.VMEM((remote, size, size), tiles.dtype)
    acc, lists = pl.pallas_call(
        own_kernel,
        out_shape=(acc_shape, jax.ShapeDtypeStruct((stripes - 1, remote), jnp.int32)),
        in_specs=[SMEM, SMEM, HBM, HBM],
        out_specs=(VMEM, SMEM),
        scratch_shapes=[
            pltpu.VMEM(x.shape, x.dtype),
            pltpu.VMEM((stripe_blocks, size, size), tiles.dtype),
            pltpu.SMEM((stripes - 1,), jnp.int32),
            pltpu.SemaphoreType.DMA((2,)),
        ],
        compiler_params=params,
        cost_estimate=pl.CostEstimate(
            flops=stripe_blocks * tile_flops, bytes_accessed=tiles.size, transcendentals=0
        ),
        name="own",
    )(me, col_block.T, in_hbm(x), in_hbm(tiles))
    ready, acc = lax.optimization_barrier((two, acc))
    three = exchange(ready, "node", stripes, 1)
    acc, three_tiles = pl.pallas_call(
        middle_kernel,
        out_shape=(acc_shape, held),
        in_specs=[VMEM, VMEM, VMEM, HBM, VMEM],
        out_specs=(VMEM, VMEM),
        input_output_aliases={4: 0},
        scratch_shapes=[
            pltpu.VMEM((3,) + held.shape, held.dtype),
            pltpu.SemaphoreType.DMA((3,)),
        ],
        compiler_params=params,
        cost_estimate=pl.CostEstimate(
            flops=2 * remote * tile_flops, bytes_accessed=tiles.size * 4, transcendentals=0
        ),
        name="middle",
    )(*in_vmem(lists, one, ready), in_hbm(tiles), *in_vmem(acc))
    part_shape = pltpu.VMEM((width, stripe_blocks // slices * size), jnp.bfloat16)
    _, *parts = pl.pallas_call(
        functools.partial(last_kernel, slot_count),
        out_shape=(acc_shape,) + (part_shape,) * slices,
        in_specs=[SMEM, VMEM, VMEM, VMEM, VMEM],
        out_specs=(VMEM,) * (1 + slices),
        input_output_aliases={4: 0},
        compiler_params=params,
        cost_estimate=pl.CostEstimate(
            flops=remote * tile_flops, bytes_accessed=tiles.size, transcendentals=0
        ),
        name="last",
    )(feat, *in_vmem(lists, three, three_tiles, acc))
    parts = [
        exchange(part, "feat", slices, slices - 1 - k) if k < slices - 1 else part
        for k, part in enumerate(parts)
    ]
    rows = part_shape.shape[1]
    classes = weight.shape[1]
    logits = pl.pallas_call(
        project_kernel,
        out_shape=jax.ShapeDtypeStruct((classes, rows), jnp.bfloat16),
        in_specs=[SMEM] + [VMEM] * (2 + slices),
        out_specs=VMEM,
        scratch_shapes=[pltpu.VMEM((slices * width, rows), jnp.bfloat16)],
        compiler_params=params,
        name="project",
    )(feat, *in_vmem(weight.T, bias[:, None], *parts))
    return logits.T


def on_device(features, tiles, col_block, weight, bias):
    stripe_blocks, slot_count, size, _ = tiles.shape
    width = features.shape[1]
    gathered = lax.all_gather(features, "node", axis=0, tiled=True)
    fetched = gathered.reshape(-1, size, width)[col_block.reshape(-1)]
    fetched = fetched.reshape(stripe_blocks, slot_count, size, width)
    summed = jnp.einsum("rkij,rkjf->rif", tiles, fetched, preferred_element_type=jnp.float32)
    aggregated = summed.astype(jnp.bfloat16).reshape(-1, width)
    rows = lax.all_to_all(aggregated, "feat", split_axis=0, concat_axis=1, tiled=True)
    logits = jnp.dot(rows, weight, preferred_element_type=jnp.float32)
    return (logits + bias).astype(jnp.bfloat16)


def solution(mesh):
    stripes, slices = mesh.shape["node"], mesh.shape["feat"]
    line = stripes == 4 and slices > 1 and slices & (slices - 1) == 0
    body = functools.partial(on_line, stripes, slices) if line else on_device
    in_specs = (
        P(("groups", "node"), "feat"),
        P(("groups", "node"), None, None, None),
        P(("groups", "node"), None),
        P(),
        P(),
    )
    out_specs = P(("groups", "node", "feat"), None)
    return jax.shard_map(
        body, mesh=mesh, in_specs=in_specs, out_specs=out_specs, check_vma=False
    )
```
